256 devices in a mesh: prompt: 8 (over x, z_lo), resp: 32 (over y, z_hi, core).
Axes of the slice: x: 4, y: 4, z: 8 (z_hi: 4, z_lo: 2; z = z_hi * 2 + z_lo), core: 2. Of those that a mesh axis runs over, the one named last changes fastest.
Arguments:
- prompt_hidden: bfloat16 [8, 2048, 5120], P('prompt', 'resp'), may hold values from -6 to 6
- prompt_keys: bfloat16 [8, 2048, 512], P('prompt', 'resp'), may hold values from -4 to 4
- prompt_values: bfloat16 [8, 2048, 512], P('prompt', 'resp'), may hold values from -6 to 6
- resp_hidden: bfloat16 [8, 32, 96, 5120], P('prompt', 'resp'), may hold values from -6 to 6
- resp_queries: bfloat16 [8, 32, 96, 4096], P('prompt', 'resp'), may hold values from -5 to 5
- resp_keys: bfloat16 [8, 32, 96, 512], P('prompt', 'resp'), may hold values from -6 to 6
- resp_values: bfloat16 [8, 32, 96, 512], P('prompt', 'resp'), may hold values from -6 to 6
- grad_out: bfloat16 [8, 32, 96, 4096], P('prompt', 'resp'), may hold values from -24 to 24
- rewards: float32 [8, 32], P('prompt', 'resp'), may hold values from -9 to 9
- lengths: int32 [8, 32], P('prompt', 'resp'), may hold values from 48 to 96, as said below
Outputs:
- grad_queries: bfloat16 [8, 32, 96, 4096], P('prompt', 'resp')
- grad_weights: float32 [5120, 1024], P(('prompt', 'resp'))
The draws below stay inside these ranges and needn't reach their ends.
Inputs may be any that keep to these rules, and one draw needn't show every extreme that they name: `lengths`: in every prompt group at least one response has the full 96 tokens.
All inputs are finite; a program needn't handle non-finite values.
Results may differ from the reference program's by a relative error of at most 0.022.
Values may be sent and summed in bfloat16 or wider, within the bound.
No kernel may reach another device: no remote copies, remote signals or barrier semaphores. Data moves between devices by JAX's collectives and lax.ppermute only.
A program may use at most 192 MiB of HBM per device.

```python
import jax
import jax.numpy as jnp
from jax import lax

D = 5120
QH = 32
KVH = 4
HD = 128
RLEN = 96
PLEN = 2048
N_PROMPT = 8
N_RESP = 32


def draw_prompt_keys(key, part):
    key = jax.random.fold_in(key, 3)
    full_shape = (N_PROMPT, PLEN, KVH * HD)
    base_draw = jax.random.truncated_normal(key, -4.0, 4.0, full_shape, jnp.float32)
    return base_draw.astype(jnp.bfloat16)


def draw_resp_queries(key, part):
    key = jax.random.fold_in(key, 4)
    full_shape = (N_PROMPT, N_RESP, RLEN, QH * HD)
    base_draw = jax.random.truncated_normal(key, -4.0, 4.0, full_shape, jnp.float32)
    return base_draw.astype(jnp.bfloat16)


def draw_rewards(key, part):
    key = jax.random.fold_in(key, 5)
    position = jnp.arange(N_RESP, dtype=jnp.float32) / (N_RESP - 1)
    scale_ramp = 1.0 / 3.0 + 2.0 / 3.0 * position
    base_draw = jax.random.truncated_normal(key, -3.0, 3.0, (N_PROMPT, N_RESP), jnp.float32)
    return base_draw * scale_ramp[None, :]


def draw_lengths(key, part):
    key = jax.random.fold_in(key, 7)
    key_lengths, key_full = jax.random.split(key)
    drawn = jax.random.randint(key_lengths, (N_PROMPT, N_RESP), RLEN // 2, RLEN + 1)
    full_index = jax.random.randint(key_full, (N_PROMPT, 1), 0, N_RESP)
    return jnp.where(jnp.arange(N_RESP)[None, :] == full_index, RLEN, drawn).astype(jnp.int32)


def with_spikes(values, key, source, target, parts, factor):
    def block_of(dim):
        return (jnp.arange(values.shape[dim]) // (values.shape[dim] // parts)).reshape((-1,) + (1,) * (values.ndim - 1 - dim))

    first = jax.random.permutation(key, parts)[block_of(target)]
    second = (block_of(target) + parts // 2) % parts
    return jnp.where((block_of(source) == first) | (block_of(source) == second), factor * values, values)


def steps_of(stream_key, extent, cuts, least, largest):
    gain, own = 1.0, jax.random.fold_in(stream_key, 6)
    for dim, shards_of in cuts:
        draws = jnp.exp(jax.random.uniform(jax.random.fold_in(own, dim), (shards_of,), jnp.float32, least / len(cuts), largest / len(cuts)))
        gain = gain * jnp.repeat(draws, extent[dim] // shards_of).reshape([-1 if axis == dim else 1 for axis in range(len(extent))])
    return gain


def gaussian(stream_key, dims, deviation, limit, cuts=(), kind=jnp.bfloat16):
    result = deviation * jax.random.normal(stream_key, dims, jnp.float32)
    if cuts:
        result = result * steps_of(stream_key, dims, cuts, -0.22, 0.18)
    return jnp.clip(result, -limit, limit).astype(kind)


def gaussian_with(key, extent, scale, limit, cuts, heavy, held_as=jnp.bfloat16):
    values = scale * jax.random.normal(key, extent, jnp.float32)
    if cuts:
        values = values * steps_of(key, extent, cuts, -0.22, 0.18)
    return jnp.clip(with_spikes(values, jax.random.fold_in(key, 3), *heavy), -limit, limit).astype(held_as)


def setup_inputs(seed: int = 0) -> dict:
    key_of = jax.random.split(jax.random.key(seed), 11)
    prompt_hidden = gaussian_with(key_of[0], (N_PROMPT, PLEN, D), 1.0, 6.0, ((0, 8), (1, 32)), (1, 2, 32, 2.75))
    prompt_keys = draw_prompt_keys(jax.random.fold_in(key_of[10], 71), 0)
    prompt_values = gaussian(key_of[2], (N_PROMPT, PLEN, KVH * HD), 1.0, 6.0, ((0, 8), (1, 32)))
    resp_hidden = gaussian_with(key_of[3], (N_PROMPT, N_RESP, RLEN, D), 1.0, 6.0, ((0, 8), (1, 32)), (1, 3, 32, 2.75))
    resp_queries = draw_resp_queries(jax.random.fold_in(key_of[10], 71), 0)
    resp_keys = gaussian(key_of[5], (N_PROMPT, N_RESP, RLEN, KVH * HD), 1.0, 6.0, ((0, 8), (1, 32)))
    resp_values = gaussian(key_of[6], (N_PROMPT, N_RESP, RLEN, KVH * HD), 1.0, 6.0, ((0, 8), (1, 32)))
    grad_out = gaussian(key_of[7], (N_PROMPT, N_RESP, RLEN, QH * HD), 4.0, 24.0, ((0, 8), (1, 32)))
    rewards = draw_rewards(jax.random.fold_in(key_of[10], 71), 0)
    lengths = draw_lengths(jax.random.fold_in(key_of[10], 71), 0)
    return {"prompt_hidden": prompt_hidden, "prompt_keys": prompt_keys, "prompt_values": prompt_values, "resp_hidden": resp_hidden, "resp_queries": resp_queries, "resp_keys": resp_keys, "resp_values": resp_values, "grad_out": grad_out, "rewards": rewards, "lengths": lengths}


def rounded(values):
    return lax.optimization_barrier(values.astype(jnp.bfloat16)).astype(jnp.float32)

def response_pass(queries, own_keys, own_values, weighted, group_keys, group_values, length):
    resp_len = queries.shape[0]
    prompt_len = group_keys.shape[0]
    group_size = QH // KVH
    factor = HD ** (-0.5)
    row_index = jnp.arange(resp_len)[:, None]
    col_index = jnp.arange(resp_len)[None, :]
    own_visible = (col_index <= row_index) & (col_index < length)
    visible = jnp.concatenate([jnp.ones((resp_len, prompt_len), dtype=bool), own_visible], axis=1)
    query_parts = []
    key_parts = []
    value_parts = []
    for kv_head in range(KVH):
        wide_cols = slice(kv_head * group_size * HD, (kv_head + 1) * group_size * HD)
        narrow = slice(kv_head * HD, (kv_head + 1) * HD)
        query_head = queries[:, wide_cols].reshape(resp_len, group_size, HD).astype(jnp.float32)
        grad_head = weighted[:, wide_cols].reshape(resp_len, group_size, HD).astype(jnp.float32)
        key_rows = jnp.concatenate([group_keys[:, narrow], own_keys[:, narrow]], axis=0).astype(jnp.float32)
        value_rows = jnp.concatenate([group_values[:, narrow], own_values[:, narrow]], axis=0).astype(jnp.float32)
        scores = jnp.einsum('igd,jd->gij', query_head, key_rows) * factor
        scores = jnp.where(visible[None], scores, -jnp.inf)
        row_top = lax.optimization_barrier(jnp.max(scores, axis=2, keepdims=True))
        expo_terms = jnp.exp(scores - row_top)
        prob_rows = rounded(expo_terms / lax.optimization_barrier(jnp.sum(expo_terms, axis=2, keepdims=True)))
        attended = jnp.einsum('gij,jd->igd', prob_rows, value_rows)
        row_delta = lax.optimization_barrier(jnp.sum(grad_head * attended, axis=2)).T[:, :, None]
        grad_prob = jnp.einsum('igd,jd->gij', grad_head, value_rows)
        dscores = rounded(prob_rows * (grad_prob - row_delta))
        query_parts.append((jnp.einsum('gij,jd->igd', dscores, key_rows) * factor).reshape(resp_len, group_size * HD))
        key_parts.append(jnp.einsum('gij,igd->jd', dscores, query_head) * factor)
        value_parts.append(jnp.einsum('gij,igd->jd', prob_rows, grad_head))
    grad_query = jnp.concatenate(query_parts, axis=1)
    key_grads = jnp.concatenate(key_parts, axis=1)
    value_grads = jnp.concatenate(value_parts, axis=1)
    prompt_part = jnp.concatenate([key_grads[:prompt_len], value_grads[:prompt_len]], axis=1)
    own_part = jnp.concatenate([key_grads[prompt_len:], value_grads[prompt_len:]], axis=1)
    return (grad_query, prompt_part, own_part)

def reference(prompt_hidden, prompt_keys, prompt_values, resp_hidden, resp_queries, resp_keys, resp_values, grad_out, rewards, lengths):
    reward_total = lax.optimization_barrier(jnp.sum(rewards, axis=1, keepdims=True))
    squares = lax.optimization_barrier(jnp.sum(rewards * rewards, axis=1, keepdims=True))
    reward_mean = reward_total / N_RESP
    spread = squares / N_RESP - reward_mean * reward_mean
    advantage = (rewards - reward_mean) / jnp.sqrt(jnp.maximum(spread, 0.5))
    weights = advantage * RLEN / lengths.astype(jnp.float32)
    kv_width = 2 * KVH * HD

    def per_group(group_args):
        keys_group, values_group, weights_group, lengths_group, queries_group, own_keys_group, own_values_group, grads_group = group_args

        def per_response(running, item):
            queries, own_keys, own_values, grads, weight, length = item
            live_rows = (jnp.arange(RLEN) < length)[:, None]
            weighted = jnp.where(live_rows, grads.astype(jnp.float32) * weight, 0.0).astype(jnp.bfloat16)
            grad_query, prompt_part, own_part = response_pass(queries, own_keys, own_values, weighted, keys_group, values_group, length)
            return (running + rounded(prompt_part), (grad_query.astype(jnp.bfloat16), own_part.astype(jnp.bfloat16)))
        running = jnp.zeros((PLEN, kv_width), jnp.float32)
        running, outputs = lax.scan(per_response, running, (queries_group, own_keys_group, own_values_group, grads_group, weights_group, lengths_group))
        return (outputs[0], running.astype(jnp.bfloat16), outputs[1])
    grad_queries, prompt_grads, own_grads = lax.map(per_group, (prompt_keys, prompt_values, weights, lengths, resp_queries, resp_keys, resp_values, grad_out))
    grad_weights = jnp.dot(prompt_hidden.reshape(-1, D).T, prompt_grads.reshape(-1, kv_width), preferred_element_type=jnp.float32)
    grad_weights = grad_weights + jnp.dot(resp_hidden.reshape(-1, D).T, own_grads.reshape(-1, kv_width), preferred_element_type=jnp.float32)
    return (grad_queries, grad_weights / (N_PROMPT * N_RESP))
```

```python
import functools

import jax
import jax.numpy as jnp
from jax import lax
from jax.experimental import pallas as pl
from jax.experimental.pallas import tpu as pltpu
from jax.sharding import Mesh, PartitionSpec as P

D = 5120
QH = 32
KVH = 4
HD = 128
RLEN = 96
PPOS = 64
GROUP = QH // KVH
ROWS = GROUP * RLEN
META = 16
NX, NZL, NY, NZH, NC = 4, 2, 4, 4, 2
N_RESP = NY * NZH * NC
DX = D // NX
KVW = 2 * HD
ZPOS = NY * PPOS
OUT_ROWS = 20
F32 = jnp.float32
BF16 = jnp.bfloat16
VMEM = pl.BlockSpec(memory_space=pltpu.VMEM)
SMEM = pl.BlockSpec(memory_space=pltpu.SMEM)


def shaped(shape, dtype):
    return jax.ShapeDtypeStruct(shape, dtype)


def call(kernel, outs, specs, cost, scratch=(), limit=48):
    flops, nbytes, trans = cost
    return pl.pallas_call(
        kernel,
        out_shape=outs,
        in_specs=specs,
        out_specs=jax.tree.map(lambda _: VMEM, outs),
        scratch_shapes=list(scratch),
        compiler_params=pltpu.CompilerParams(vmem_limit_bytes=limit * 1024 * 1024),
        cost_estimate=pl.CostEstimate(flops=flops, bytes_accessed=nbytes, transcendentals=trans),
    )


def pack_kv_kernel(y_ref, rw_ref, ln_ref, pk_ref, pv_ref, rk_ref, rv_ref, *outs):
    y = y_ref[0]
    reward = jnp.full((META, HD), rw_ref[0, 0], F32)
    high = reward.astype(BF16)
    rest = reward - high.astype(F32)
    mid = rest.astype(BF16)
    low = rest - mid.astype(F32)
    lane = lax.broadcasted_iota(jnp.int32, (META, HD), 1)
    length = jnp.full((META, HD), ln_ref[0, 0].astype(F32), F32)
    meta = jnp.where(lane == 0, high.astype(F32), 0.0)
    meta = jnp.where(lane == 1, mid.astype(F32), meta)
    meta = jnp.where(lane == 2, low, meta)
    meta = jnp.where(lane == 3, length, meta).astype(BF16)
    for k in range(NY):
        cols = pl.ds(pl.multiple_of(lax.rem(y + k, NY) * HD, HD), HD)
        out = outs[k]
        out[0:PPOS, 0:HD] = pk_ref[0, :, cols]
        out[0:PPOS, HD:KVW] = pv_ref[0, :, cols]
        out[PPOS:PPOS + RLEN, 0:HD] = rk_ref[0, 0, :, cols]
        out[PPOS:PPOS + RLEN, HD:KVW] = rv_ref[0, 0, :, cols]
        out[PPOS + RLEN:, 0:HD] = meta
        out[PPOS + RLEN:, HD:KVW] = meta


def pack_qd_kernel(y_ref, q_ref, g_ref, *outs):
    y = y_ref[0]
    wide = GROUP * HD
    for k in range(NY):
        cols = pl.ds(pl.multiple_of(lax.rem(y + k, NY) * wide, HD), wide)
        outs[k][0:RLEN, :] = q_ref[0, 0, :, cols]
        outs[k][RLEN:, :] = g_ref[0, 0, :, cols]


def pack_hidden_kernel(x_ref, ph_ref, rh_ref, *outs):
    x = x_ref[0]
    for k in range(NX):
        cols = pl.ds(pl.multiple_of(lax.rem(x + k, NX) * DX, HD), DX)
        outs[k][0:PPOS, :] = ph_ref[0, :, cols]
        outs[k][PPOS:, :] = rh_ref[0, 0, :, cols]


def pack_z_kernel(*refs):
    ins, out = refs[:NY], refs[NY]
    row = lax.broadcasted_iota(jnp.int32, (META, KVW), 0)
    meta = jnp.zeros((META, KVW), F32)
    for k in range(NY):
        out[k * PPOS:(k + 1) * PPOS, :] = ins[k][0:PPOS, :]
        meta = jnp.where(row == k, ins[k][PPOS + RLEN:, :].astype(F32), meta)
    out[ZPOS:, :] = meta.astype(BF16)


def nt(a, b):
    return lax.dot_general(a, b, (((1,), (1,)), ((), ())), preferred_element_type=F32)


def nn(a, b):
    return lax.dot_general(a, b, (((1,), (0,)), ((), ())), preferred_element_type=F32)


def tn(a, b):
    return lax.dot_general(a, b, (((0,), (0,)), ((), ())), preferred_element_type=F32)


NT = 2 * NZH


def attention_kernel(*refs):
    kv = refs[0:NT]
    own = refs[NT:NT + NY]
    qd = refs[NT + NY:NT + 2 * NY]
    dq_refs = refs[NT + 2 * NY:NT + 3 * NY]
    gown_ref, gmine_ref, gother_ref = refs[NT + 3 * NY:NT + 3 * NY + 3]
    s_ref, dp_ref, q_ref, do_ref, kt_ref, acc_ref = refs[NT + 3 * NY + 3:]
    scale = HD ** (-0.5)
    log2e = 1.4426950408889634

    lane = lax.broadcasted_iota(jnp.int32, (META, HD), 1)
    row = lax.broadcasted_iota(jnp.int32, (META, HD), 0)
    total = jnp.zeros((1, 1), F32)
    squares = jnp.zeros((1, 1), F32)
    for t in range(NT):
        meta = kv[t][ZPOS:, 0:HD].astype(F32)
        rewards = jnp.sum(jnp.where((lane < 3) & (row < NY), meta, 0.0), axis=1, keepdims=True)
        total = total + jnp.sum(rewards, axis=0, keepdims=True)
        squares = squares + jnp.sum(rewards * rewards, axis=0, keepdims=True)
    mean = total / N_RESP
    spread = squares / N_RESP - mean * mean
    inverse = 1.0 / jnp.sqrt(jnp.maximum(spread, 0.5))

    for t in range(NT):
        kt_ref[:, t * ZPOS:(t + 1) * ZPOS] = kv[t][0:ZPOS, 0:HD].T

    own_start = NT * ZPOS
    key_index = lax.broadcasted_iota(jnp.int32, (RLEN, ROWS), 0)
    row_index = lax.rem(lax.broadcasted_iota(jnp.int32, (RLEN, ROWS), 1), RLEN)
    position = lax.broadcasted_iota(jnp.int32, (RLEN, HD), 0).astype(F32)

    for j in range(NY):
        meta = own[j][PPOS + RLEN:, 0:HD].astype(F32)
        reward = jnp.sum(jnp.where(lane < 3, meta, 0.0), axis=1, keepdims=True)[0:1]
        length = jnp.sum(jnp.where(lane == 3, meta, 0.0), axis=1, keepdims=True)[0:1]
        weight = (reward - mean) * inverse * RLEN / length
        live = position < length
        for h in range(GROUP):
            cols = slice(h * HD, (h + 1) * HD)
            rows = slice(h * RLEN, (h + 1) * RLEN)
            q_ref[rows, :] = qd[j][0:RLEN, cols]
            grad = qd[j][RLEN:2 * RLEN, cols].astype(F32)
            do_ref[rows, :] = jnp.where(live, grad * weight, 0.0).astype(BF16)
        kt_ref[:, own_start:own_start + RLEN] = own[j][PPOS:PPOS + RLEN, 0:HD].T
        q = q_ref[...]
        do = do_ref[...]
        mask = (key_index <= row_index) & (key_index.astype(F32) < length)

        tiles = [(kv[t], 0, ZPOS, t * ZPOS) for t in range(NT)]
        tiles.append((own[j], PPOS, RLEN, own_start))
        top = None
        for ref, start, size, at in tiles:
            s = nt(ref[start:start + size, 0:HD], q)
            if at == own_start:
                s = jnp.where(mask, s, -jnp.inf)
            s_ref[at:at + size, :] = s
            part = jnp.max(s, axis=0, keepdims=True)
            top = part if top is None else jnp.maximum(top, part)
        factor = scale * log2e
        top = top * factor
        norm = jnp.zeros((1, ROWS), F32)
        delta = jnp.zeros((1, ROWS), F32)
        for ref, start, size, at in tiles:
            p = jnp.exp2(s_ref[at:at + size, :] * factor - top)
            s_ref[at:at + size, :] = p
            dp = nt(ref[start:start + size, HD:KVW], do)
            dp_ref[at:at + size, :] = dp
            norm = norm + jnp.sum(p, axis=0, keepdims=True)
            delta = delta + jnp.sum(p * dp, axis=0, keepdims=True)
        inv = 1.0 / norm
        delta = delta * inv
        dq = jnp.zeros((HD, ROWS), F32)
        for ref, start, size, at in tiles:
            p = s_ref[at:at + size, :] * inv
            ds = (p * (dp_ref[at:at + size, :] - delta)).astype(BF16)
            dk = nn(ds, q) * scale
            dv = nn(p.astype(BF16), do)
            dq = dq + nn(kt_ref[:, at:at + size], ds)
            if at == own_start:
                gown_ref[j * RLEN:(j + 1) * RLEN, 0:HD] = dk.astype(BF16)
                gown_ref[j * RLEN:(j + 1) * RLEN, HD:KVW] = dv.astype(BF16)
            elif j == 0:
                acc_ref[at:at + size, 0:HD] = dk
                acc_ref[at:at + size, HD:KVW] = dv
            else:
                acc_ref[at:at + size, 0:HD] += dk
                acc_ref[at:at + size, HD:KVW] += dv
        dq = (dq * scale).T
        for h in range(GROUP):
            dq_refs[j][:, h * HD:(h + 1) * HD] = dq[h * RLEN:(h + 1) * RLEN, :].astype(BF16)
    half = NZH * ZPOS
    gmine_ref[...] = acc_ref[0:half, :].astype(BF16)
    gother_ref[...] = acc_ref[half:, :].astype(BF16)


def attention(kv, own, qd):
    keys = NT * ZPOS + RLEN
    pairs = NY * ROWS * keys
    outs = [shaped((RLEN, GROUP * HD), BF16)] * NY + [
        shaped((NY * RLEN, KVW), BF16),
        shaped((NZH * ZPOS, KVW), BF16),
        shaped((NZH * ZPOS, KVW), BF16),
    ]
    scratch = [
        pltpu.VMEM((keys, ROWS), F32),
        pltpu.VMEM((keys, ROWS), F32),
        pltpu.VMEM((ROWS, HD), BF16),
        pltpu.VMEM((ROWS, HD), BF16),
        pltpu.VMEM((HD, keys + 32), BF16),
        pltpu.VMEM((NT * ZPOS, KVW), F32),
    ]
    return call(
        attention_kernel, outs, [VMEM] * (NT + 2 * NY), (pairs * HD * 10 * 2, 6 << 20, pairs), scratch
    )(*kv, *own, *qd)


def core_sum_kernel(mine_ref, got_ref, *outs):
    for k in range(NZH):
        rows = slice(k * ZPOS, (k + 1) * ZPOS)
        outs[k][...] = (mine_ref[rows, :].astype(F32) + got_ref[rows, :].astype(F32)).astype(BF16)


def sum_kernel(*refs):
    ins, out = refs[:-1], refs[-1]
    total = ins[0][...].astype(F32)
    for ref in ins[1:]:
        total = total + ref[...].astype(F32)
    out[...] = total.astype(out.dtype)


def own_weight_kernel(*refs):
    hidden = refs[0:2 * NY]
    grads = refs[2 * NY:2 * NY + NX]
    acc_ref, prompt_ref = refs[2 * NY + NX:2 * NY + NX + 2]
    own_ref = refs[2 * NY + NX + 2]
    block = PPOS + RLEN
    for i in range(NX):
        for j in range(NY):
            ref = hidden[2 * j + i // 2]
            at = (i % 2) * block
            prompt_ref[i * ZPOS + j * PPOS:i * ZPOS + (j + 1) * PPOS, :] = ref[at:at + PPOS, :]
            own_ref[j * RLEN:(j + 1) * RLEN, :] = ref[at + PPOS:at + block, :]
        term = tn(grads[i][...], own_ref[...])
        if i == 0:
            acc_ref[...] = term
        else:
            acc_ref[...] += term


def prompt_weight_kernel(c_ref, acc_ref, hidden_ref, *refs):
    grads = refs[:NX]
    mine_ref, send_ref = refs[NX:]
    total = acc_ref[...]
    for i in range(NX):
        total = total + tn(grads[i][...], hidden_ref[i * ZPOS:(i + 1) * ZPOS, :])
    total = total.T
    first = c_ref[0] == 0
    for zl in range(NZL):
        for zh in range(NZH):
            parts = []
            for c in range(NC):
                pieces = []
                for y in range(NY):
                    at = (((zl * NY + y) * NZH + zh) * NC + c) * OUT_ROWS
                    pieces.append(total[at:at + OUT_ROWS, :])
                parts.append(jnp.concatenate(pieces, axis=0))
            mine_ref[zl * NZH + zh] = jnp.where(first, parts[0], parts[1])
            send_ref[zl * NZH + zh] = jnp.where(first, parts[1], parts[0]).astype(send_ref.dtype)


def core_weight_kernel(z_ref, mine_ref, got_ref, *outs):
    zl, zh = z_ref[0], z_ref[1]
    for a in range(NZL):
        for k in range(NZH):
            at = lax.rem(zl + a, NZL) * NZH + lax.rem(zh + k, NZH)
            outs[a * NZH + k][...] = (mine_ref[at] + got_ref[at].astype(F32)).astype(BF16)


def chip_weight_kernel(y_ref, *refs):
    ins, outs = refs[:NZL * NZH], refs[NZL * NZH:]
    y = y_ref[0]
    total = ins[0][...].astype(F32)
    for ref in ins[1:]:
        total = total + ref[...].astype(F32)
    total = total * (1.0 / (NX * NZL * N_RESP))
    chunks = [total[i * OUT_ROWS:(i + 1) * OUT_ROWS, :] for i in range(NY)]
    for k in range(NY):
        want = lax.rem(y + k, NY)
        chosen = chunks[0]
        for i in range(1, NY):
            chosen = jnp.where(want == i, chunks[i], chosen)
        outs[k][...] = chosen


def final_kernel(y_ref, *refs):
    ins, out = refs[:NY], refs[NY]
    y = y_ref[0]
    for k in range(NY):
        at = lax.rem(y + NY - k, NY) * HD
        out[:, pl.ds(pl.multiple_of(at, HD), HD)] = ins[k][:, 0:HD]
        out[:, pl.ds(pl.multiple_of(at + KVH * HD, HD), HD)] = ins[k][:, HD:KVW]


def queries_kernel(y_ref, *refs):
    ins, out = refs[:NY], refs[NY]
    y = y_ref[0]
    wide = GROUP * HD
    for k in range(NY):
        at = lax.rem(y + k, NY) * wide
        out[0, 0, :, pl.ds(pl.multiple_of(at, HD), wide)] = ins[k][...]


def shift(value, axis, size, step):
    if step % size == 0:
        return value
    return lax.ppermute(value, axis, [(i, (i + step) % size) for i in range(size)])


def swap(value):
    return shift(value, "c", NC, 1)


def z_shift(value, a, k):
    if a == 0 and k == 0:
        return value
    pairs = [
        (zl * NZH + zh, ((zl + a) % NZL) * NZH + (zh + k) % NZH)
        for zl in range(NZL)
        for zh in range(NZH)
    ]
    return lax.ppermute(value, ("zl", "zh"), pairs)


def body(ph, pk, pv, rh, rq, rk, rv, go, rw, ln):
    index = lambda name: lax.axis_index(name).astype(jnp.int32).reshape(1)
    x, y, c = index("x"), index("y"), index("c")
    z = jnp.concatenate([index("zl"), index("zh")])
    small = (0, 1 << 20, 0)

    packs = call(
        pack_kv_kernel,
        [shaped((PPOS + RLEN + META, KVW), BF16)] * NY,
        [SMEM] * 3 + [VMEM] * 4,
        small,
    )(y, rw, ln, pk, pv, rk, rv)
    own = [shift(packs[k], "y", NY, k) for k in range(NY)]
    qd_packs = call(
        pack_qd_kernel, [shaped((2 * RLEN, GROUP * HD), BF16)] * NY, [SMEM, VMEM, VMEM], small
    )(y, rq, go)
    qd = [shift(qd_packs[k], "y", NY, k) for k in range(NY)]
    kvz = call(pack_z_kernel, shaped((ZPOS + META, KVW), BF16), [VMEM] * NY, small)(*own)
    zpieces = [shift(kvz, "zh", NZH, k) for k in range(NZH)]
    cpieces = [swap(piece) for piece in zpieces]

    hidden_packs = call(
        pack_hidden_kernel, [shaped((PPOS + RLEN, DX), BF16)] * NX, [SMEM, VMEM, VMEM], small
    )(x, ph, rh)
    hx = [shift(hidden_packs[k], "x", NX, k) for k in range(NX)]
    ha = jnp.concatenate(hx[0:2], axis=0)
    hb = jnp.concatenate(hx[2:4], axis=0)
    ha_left, ha_right = shift(ha, "y", NY, 1), shift(ha, "y", NY, -1)
    hb_left, hb_right = shift(hb, "y", NY, 1), shift(hb, "y", NY, -1)
    ha_far = shift(ha_left, "y", NY, 1)
    hb_far = shift(hb_right, "y", NY, -1)
    hidden = [ha, hb, ha_left, hb_left, ha_far, hb_far, ha_right, hb_right]

    *dq, gown, gmine, gother = attention(zpieces + cpieces, own, qd)
    got = swap(gother)
    gown_x = [shift(gown, "x", NX, k) for k in range(NX)]
    sums = call(core_sum_kernel, [shaped((ZPOS, KVW), BF16)] * NZH, [VMEM] * 2, small)(gmine, got)
    back = [shift(sums[k], "zh", NZH, -k) for k in range(NZH)]
    gprompt = call(sum_kernel, shaped((ZPOS, KVW), BF16), [VMEM] * NZH, small)(*back)
    gprompt_x = [shift(gprompt, "x", NX, k) for k in range(NX)]

    dq_back = [shift(dq[k], "y", NY, -k) for k in range(NY)]
    grad_queries = call(
        queries_kernel, shaped((1, 1, RLEN, QH * HD), BF16), [SMEM] + [VMEM] * NY, small
    )(y, *dq_back)

    acc, prompt_hidden = call(
        own_weight_kernel,
        [shaped((KVW, DX), F32), shaped((NX * ZPOS, DX), BF16)],
        [VMEM] * (2 * NY + NX),
        (2 * NX * NY * RLEN * DX * KVW, 10 << 20, 0),
        [pltpu.VMEM((NY * RLEN, DX), BF16)],
    )(*hidden, *gown_x)
    chunk = NY * OUT_ROWS
    mine, send = call(
        prompt_weight_kernel,
        [shaped((NZL * NZH, chunk, KVW), F32), shaped((NZL * NZH, chunk, KVW), BF16)],
        [SMEM] + [VMEM] * (2 + NX),
        (2 * NX * ZPOS * DX * KVW, 4 << 20, 0),
    )(c, acc, prompt_hidden, *gprompt_x)
    got = swap(send)
    parts = call(
        core_weight_kernel, [shaped((chunk, KVW), BF16)] * (NZL * NZH), [SMEM] + [VMEM] * 2, small
    )(z, mine, got)
    parts = [z_shift(parts[a * NZH + k], a, k) for a in range(NZL) for k in range(NZH)]
    pieces = call(
        chip_weight_kernel, [shaped((OUT_ROWS, KVW), F32)] * NY, [SMEM] + [VMEM] * (NZL * NZH), small
    )(y, *parts)
    pieces = [shift(pieces[k], "y", NY, k) for k in range(NY)]
    grad_weights = call(
        final_kernel, shaped((OUT_ROWS, 2 * KVH * HD), F32), [SMEM] + [VMEM] * NY, small
    )(y, *pieces)
    return grad_queries, grad_weights


def solution(mesh):
    inner = Mesh(mesh.devices.reshape(NX, NZL, NY, NZH, NC), ("x", "zl", "y", "zh", "c"))
    prompt, resp = ("x", "zl"), ("y", "zh", "c")
    three, four = P(prompt, resp, None), P(prompt, resp, None, None)
    return jax.shard_map(
        body,
        mesh=inner,
        in_specs=(three, three, three, four, four, four, four, four, P(prompt, resp), P(prompt, resp)),
        out_specs=(four, P(prompt + resp, None)),
        check_vma=False,
    )
```

```python
import functools

import jax
import jax.numpy as jnp
from jax import lax
from jax.experimental import pallas as pl
from jax.experimental.pallas import tpu as pltpu
from jax.sharding import Mesh, PartitionSpec as P

D = 5120
QH = 32
KVH = 4
HD = 128
RLEN = 96
PPOS = 64
GROUP = QH // KVH
ROWS = GROUP * RLEN
META = 16
NX, NZL, NY, NZH, NC = 4, 2, 4, 4, 2
N_RESP = NY * NZH * NC
DX = D // NX
KVW = 2 * HD
ZPOS = NY * PPOS
OUT_ROWS = 20
F32 = jnp.float32
BF16 = jnp.bfloat16
VMEM = pl.BlockSpec(memory_space=pltpu.VMEM)
SMEM = pl.BlockSpec(memory_space=pltpu.SMEM)


def shaped(shape, dtype):
    return jax.ShapeDtypeStruct(shape, dtype)


def call(kernel, outs, specs, cost, scratch=(), limit=28):
    flops, nbytes, trans = cost
    return pl.pallas_call(
        kernel,
        name=kernel.__name__.replace("_kernel", ""),
        out_shape=outs,
        in_specs=specs,
        out_specs=jax.tree.map(lambda _: VMEM, outs),
        scratch_shapes=list(scratch),
        compiler_params=pltpu.CompilerParams(vmem_limit_bytes=limit * 1024 * 1024),
        cost_estimate=pl.CostEstimate(flops=flops, bytes_accessed=nbytes, transcendentals=trans),
    )


def pack_kernel(y_ref, rw_ref, ln_ref, pk_ref, pv_ref, rk_ref, rv_ref, q_ref, g_ref, *refs):
    kv, qd, sem = refs[:NY], refs[NY:2 * NY], refs[2 * NY]
    y = y_ref[0]
    wide = GROUP * HD
    low, high = pl.ds(0, HD), pl.ds(HD, HD)
    copies = []

    def copy(source, target):
        moved = pltpu.make_async_copy(source, target, sem.at[len(copies)])
        moved.start()
        copies.append(moved)

    for k in (1, 3, 2, 0):
        cols = pl.ds(pl.multiple_of(lax.rem(y + k, NY) * HD, HD), HD)
        copy(pk_ref.at[0, :, cols], kv[k].at[pl.ds(0, PPOS), low])
        copy(pv_ref.at[0, :, cols], kv[k].at[pl.ds(0, PPOS), high])
        copy(rk_ref.at[0, 0, :, cols], kv[k].at[pl.ds(PPOS, RLEN), low])
        copy(rv_ref.at[0, 0, :, cols], kv[k].at[pl.ds(PPOS, RLEN), high])
    for k in (1, 3, 2, 0):
        cols = pl.ds(pl.multiple_of(lax.rem(y + k, NY) * wide, HD), wide)
        copy(q_ref.at[0, 0, :, cols], qd[k].at[pl.ds(0, RLEN), :])
        copy(g_ref.at[0, 0, :, cols], qd[k].at[pl.ds(RLEN, RLEN), :])
    reward = jnp.full((META, KVW), rw_ref[0, 0], F32)
    top = reward.astype(BF16)
    rest = reward - top.astype(F32)
    mid = rest.astype(BF16)
    tail = rest - mid.astype(F32)
    lane = lax.broadcasted_iota(jnp.int32, (META, KVW), 1)
    length = jnp.full((META, KVW), ln_ref[0, 0].astype(F32), F32)
    meta = jnp.where(lane == 0, top.astype(F32), 0.0)
    meta = jnp.where(lane == 1, mid.astype(F32), meta)
    meta = jnp.where(lane == 2, tail, meta)
    meta = jnp.where(lane == 3, length, meta).astype(BF16)
    for k in range(NY):
        kv[k][PPOS + RLEN:, :] = meta
    for moved in copies:
        moved.wait()


def pack_z_kernel(*refs):
    ins, out = refs[:NY], refs[NY]
    row = lax.broadcasted_iota(jnp.int32, (META, KVW), 0)
    meta = jnp.zeros((META, KVW), F32)
    for k in range(NY):
        out[k * PPOS:(k + 1) * PPOS, :] = ins[k][0:PPOS, :]
        meta = jnp.where(row == k, ins[k][PPOS + RLEN:, :].astype(F32), meta)
    out[ZPOS:, :] = meta.astype(BF16)


def nt(a, b):
    return lax.dot_general(a, b, (((1,), (1,)), ((), ())), preferred_element_type=F32)


def nn(a, b):
    return lax.dot_general(a, b, (((1,), (0,)), ((), ())), preferred_element_type=F32)


def tn(a, b):
    return lax.dot_general(a, b, (((0,), (0,)), ((), ())), preferred_element_type=F32)


NT = 2 * NZH


def attention_kernel(*refs):
    kv = refs[0:NT]
    own = refs[NT:NT + NY]
    qd = refs[NT + NY:NT + 2 * NY]
    dq_refs = refs[NT + 2 * NY:NT + 3 * NY]
    gown_ref, gmine_ref, gother_ref = refs[NT + 3 * NY:NT + 3 * NY + 3]
    s_ref, dp_ref, q_ref, do_ref, kt_ref, acc_ref = refs[NT + 3 * NY + 3:]
    scale = HD ** (-0.5)
    log2e = 1.4426950408889634

    lane = lax.broadcasted_iota(jnp.int32, (META, HD), 1)
    row = lax.broadcasted_iota(jnp.int32, (META, HD), 0)
    total = jnp.zeros((1, 1), F32)
    squares = jnp.zeros((1, 1), F32)
    for t in range(NT):
        meta = kv[t][ZPOS:, 0:HD].astype(F32)
        rewards = jnp.sum(jnp.where((lane < 3) & (row < NY), meta, 0.0), axis=1, keepdims=True)
        total = total + jnp.sum(rewards, axis=0, keepdims=True)
        squares = squares + jnp.sum(rewards * rewards, axis=0, keepdims=True)
    mean = total / N_RESP
    spread = squares / N_RESP - mean * mean
    inverse = 1.0 / jnp.sqrt(jnp.maximum(spread, 0.5))

    for t in range(NT):
        kt_ref[:, t * ZPOS:(t + 1) * ZPOS] = kv[t][0:ZPOS, 0:HD].T

    own_start = NT * ZPOS
    key_index = lax.broadcasted_iota(jnp.int32, (RLEN, ROWS), 0)
    row_index = lax.rem(lax.broadcasted_iota(jnp.int32, (RLEN, ROWS), 1), RLEN)
    position = lax.broadcasted_iota(jnp.int32, (RLEN, HD), 0).astype(F32)

    for j in range(NY):
        meta = own[j][PPOS + RLEN:, 0:HD].astype(F32)
        reward = jnp.sum(jnp.where(lane < 3, meta, 0.0), axis=1, keepdims=True)[0:1]
        length = jnp.sum(jnp.where(lane == 3, meta, 0.0), axis=1, keepdims=True)[0:1]
        weight = (reward - mean) * inverse * RLEN / length
        live = position < length
        for h in range(GROUP):
            cols = slice(h * HD, (h + 1) * HD)
            rows = slice(h * RLEN, (h + 1) * RLEN)
            q_ref[rows, :] = qd[j][0:RLEN, cols]
            grad = qd[j][RLEN:2 * RLEN, cols].astype(F32)
            do_ref[rows, :] = jnp.where(live, grad * weight, 0.0).astype(BF16)
        kt_ref[:, own_start:own_start + RLEN] = own[j][PPOS:PPOS + RLEN, 0:HD].T
        q = q_ref[...]
        do = do_ref[...]
        mask = (key_index <= row_index) & (key_index.astype(F32) < length)

        tiles = [(kv[t], 0, ZPOS, t * ZPOS) for t in range(NT)]
        tiles.append((own[j], PPOS, RLEN, own_start))
        top = None
        for ref, start, size, at in tiles:
            s = nt(ref[start:start + size, 0:HD], q)
            if at == own_start:
                s = jnp.where(mask, s, -jnp.inf)
            s_ref[at:at + size, :] = s
            part = jnp.max(s, axis=0, keepdims=True)
            top = part if top is None else jnp.maximum(top, part)
        factor = scale * log2e
        top = top * factor
        norm = jnp.zeros((1, ROWS), F32)
        delta = jnp.zeros((1, ROWS), F32)
        for ref, start, size, at in tiles:
            p = jnp.exp2(s_ref[at:at + size, :] * factor - top)
            s_ref[at:at + size, :] = p
            dp = nt(ref[start:start + size, HD:KVW], do)
            dp_ref[at:at + size, :] = dp
            norm = norm + jnp.sum(p, axis=0, keepdims=True)
            delta = delta + jnp.sum(p * dp, axis=0, keepdims=True)
        inv = 1.0 / norm
        delta = delta * inv
        dq = jnp.zeros((HD, ROWS), F32)
        for ref, start, size, at in tiles:
            p = s_ref[at:at + size, :] * inv
            ds = (p * (dp_ref[at:at + size, :] - delta)).astype(BF16)
            dk = nn(ds, q) * scale
            dv = nn(p.astype(BF16), do)
            dq = dq + nn(kt_ref[:, at:at + size], ds)
            if at == own_start:
                gown_ref[j * RLEN:(j + 1) * RLEN, 0:HD] = dk.astype(BF16)
                gown_ref[j * RLEN:(j + 1) * RLEN, HD:KVW] = dv.astype(BF16)
            elif j == 0:
                acc_ref[at:at + size, 0:HD] = dk
                acc_ref[at:at + size, HD:KVW] = dv
            else:
                acc_ref[at:at + size, 0:HD] += dk
                acc_ref[at:at + size, HD:KVW] += dv
        dq = (dq * scale).T
        for h in range(GROUP):
            dq_refs[j][:, h * HD:(h + 1) * HD] = dq[h * RLEN:(h + 1) * RLEN, :].astype(BF16)
    half = NZH * ZPOS
    gmine_ref[...] = acc_ref[0:half, :].astype(BF16)
    gother_ref[...] = acc_ref[half:, :].astype(BF16)


def attention(kv, own, qd):
    keys = NT * ZPOS + RLEN
    pairs = NY * ROWS * keys
    outs = [shaped((RLEN, GROUP * HD), BF16)] * NY + [
        shaped((NY * RLEN, KVW), BF16),
        shaped((NZH * ZPOS, KVW), BF16),
        shaped((NZH * ZPOS, KVW), BF16),
    ]
    scratch = [
        pltpu.VMEM((keys, ROWS), F32),
        pltpu.VMEM((keys, ROWS), F32),
        pltpu.VMEM((ROWS, HD), BF16),
        pltpu.VMEM((ROWS, HD), BF16),
        pltpu.VMEM((HD, keys + 32), BF16),
        pltpu.VMEM((NT * ZPOS, KVW), F32),
    ]
    return call(
        attention_kernel, outs, [VMEM] * (NT + 2 * NY), (pairs * HD, 6 << 20, 0), scratch
    )(*kv, *own, *qd)


def core_sum_kernel(mine_ref, got_ref, *outs):
    for k in range(NZH):
        rows = slice(k * ZPOS, (k + 1) * ZPOS)
        outs[k][...] = (mine_ref[rows, :].astype(F32) + got_ref[rows, :].astype(F32)).astype(BF16)


def sum_kernel(*refs):
    ins, out = refs[:-1], refs[-1]
    total = ins[0][...].astype(F32)
    for ref in ins[1:]:
        total = total + ref[...].astype(F32)
    out[...] = total.astype(out.dtype)


HALF = (PPOS + RLEN) // 2


def own_weight_kernel(here_ref, left_ref, far_low_ref, far_high_ref, right_ref, grads_ref, acc_ref, prompt_ref, own_ref):
    low = HALF - PPOS
    for k, ref in ((0, here_ref), (1, left_ref), (3, right_ref)):
        own_ref[k * RLEN:(k + 1) * RLEN, :] = ref[PPOS:, :]
        prompt_ref[k * PPOS:(k + 1) * PPOS, :] = ref[0:PPOS, :]
    own_ref[2 * RLEN:2 * RLEN + low, :] = far_low_ref[PPOS:, :]
    own_ref[2 * RLEN + low:3 * RLEN, :] = far_high_ref[...]
    prompt_ref[2 * PPOS:3 * PPOS, :] = far_low_ref[0:PPOS, :]
    grads = grads_ref[...]
    for i in range(NX):
        cols = slice(i * DX, (i + 1) * DX)
        acc_ref[:, cols] = tn(grads, own_ref[:, cols])


def prompt_weight_kernel(c_ref, acc_ref, hidden_ref, grads_ref, mine_ref, send_ref):
    first = c_ref[0] == 0
    grads = grads_ref[...]
    for i in range(NX):
        cols = slice(i * DX, (i + 1) * DX)
        total = acc_ref[:, cols] + tn(grads, hidden_ref[:, cols])
        low, high = total[0:HD], total[HD:KVW]
        mine_ref[:, cols] = jnp.where(first, low, high)
        send_ref[:, cols] = jnp.where(first, high, low).astype(BF16)


SPLIT = NX * NZL
DZ = D // SPLIT


def core_weight_kernel(mine_ref, got_ref, out):
    for k in range(SPLIT):
        cols = slice(k * DZ, (k + 1) * DZ)
        out[k * HD:(k + 1) * HD, :] = (mine_ref[:, cols] + got_ref[:, cols].astype(F32)).astype(BF16)


PAIR = NC * OUT_ROWS


def row_weight_kernel(in_ref, out):
    total = in_ref[0:HD, :].astype(F32)
    for i in range(1, SPLIT):
        total = total + in_ref[i * HD:(i + 1) * HD, :].astype(F32)
    out[...] = total.T.astype(BF16)


def head_weight_kernel(c_ref, in_ref, mine_ref, send_ref):
    first = c_ref[0] == 0
    terms = in_ref[...].astype(F32)
    for h in range(NY):
        total = jnp.zeros((PAIR, HD), F32)
        for zh in range(NZH):
            at = (h * NZH + zh) * PAIR
            total = total + terms[at:at + PAIR, :]
        total = total * (1.0 / (NX * NZL * N_RESP))
        low, high = total[0:OUT_ROWS, :], total[OUT_ROWS:PAIR, :]
        cols = slice(h * HD, (h + 1) * HD)
        mine_ref[:, cols] = jnp.where(first, low, high)
        send_ref[:, cols] = jnp.where(first, high, low)


def final_kernel(c_ref, mine_ref, got_ref, out):
    first = c_ref[0] == 0
    mine, got = mine_ref[...], got_ref[...]
    out[:, 0:KVH * HD] = jnp.where(first, mine, got)
    out[:, KVH * HD:] = jnp.where(first, got, mine)


def queries_kernel(y_ref, *refs):
    ins, out = refs[:NY], refs[NY]
    y = y_ref[0]
    wide = GROUP * HD
    for k in range(NY):
        at = lax.rem(y + k, NY) * wide
        out[0, 0, :, pl.ds(pl.multiple_of(at, HD), wide)] = ins[k][...]


def shift(value, axis, size, step):
    if step % size == 0:
        return value
    return lax.ppermute(value, axis, [(i, (i + step) % size) for i in range(size)])


def swap(value):
    return shift(value, "c", NC, 1)


def body(ph, pk, pv, rh, rq, rk, rv, go, rw, ln):
    index = lambda name: lax.axis_index(name).astype(jnp.int32).reshape(1)
    y, c = index("y"), index("c")
    after = lambda values, *others: lax.optimization_barrier((values, others))[0]
    small = (0, 1 << 20, 0)

    packs = call(
        pack_kernel,
        [shaped((PPOS + RLEN + META, KVW), BF16)] * NY + [shaped((2 * RLEN, GROUP * HD), BF16)] * NY,
        [SMEM] * 3 + [pl.BlockSpec(memory_space=pltpu.HBM)] * 6,
        small,
        [pltpu.SemaphoreType.DMA((6 * NY,))],
        limit=58,
    )(y, rw, ln, pk, pv, rk, rv, rq, go)
    kv_packs, qd_packs = packs[:NY], packs[NY:]
    own = [shift(kv_packs[k], "y", NY, k) for k in range(NY)]
    qd = [shift(qd_packs[k], "y", NY, k) if k != 2 else None for k in range(NY)]
    kvz = call(pack_z_kernel, shaped((ZPOS + META, KVW), BF16), [VMEM] * NY, small)(
        *after(own, qd[1], qd[3])
    )
    zpieces = [shift(kvz, "zh", NZH, k) for k in range(NZH)]
    qd[2] = shift(after(qd_packs[2], own, qd[1], qd[3]), "y", NY, 2)
    cpieces = [swap(piece) for piece in zpieces]
    hidden = jnp.concatenate([ph[0], rh[0, 0]], axis=0)
    ready = after(hidden, qd[2], zpieces[1:])
    left, right = shift(ready, "y", NY, 1), shift(ready, "y", NY, -1)

    *dq, gown, gmine, gother = attention(zpieces + cpieces, own, qd)
    left, right = after((left, right), gother)
    far_low = shift(left[:HALF], "y", NY, 1)
    far_high = shift(right[HALF:], "y", NY, -1)
    got = swap(gother)
    sums = call(core_sum_kernel, [shaped((ZPOS, KVW), BF16)] * NZH, [VMEM] * 2, small)(gmine, got)
    back = [shift(sums[k], "zh", NZH, -k) for k in range(NZH)]
    acc, prompt_hidden = call(
        own_weight_kernel,
        [shaped((KVW, D), F32), shaped((ZPOS, D), BF16)],
        [VMEM] * 6,
        (2 * NY * RLEN * D * KVW, 12 << 20, 0),
        [pltpu.VMEM((NY * RLEN, D), BF16)],
    )(hidden, left, far_low, far_high, right, gown)
    gprompt = call(sum_kernel, shaped((ZPOS, KVW), BF16), [VMEM] * NZH, small)(*after(back, acc))

    dq_back = [shift(dq[k] if k != 2 else after(dq[k], gprompt), "y", NY, -k) for k in range(NY)]
    grad_queries = call(
        queries_kernel, shaped((1, 1, RLEN, QH * HD), BF16), [SMEM] + [VMEM] * NY, small
    )(y, *dq_back)

    mine, send = call(
        prompt_weight_kernel,
        [shaped((HD, D), F32), shaped((HD, D), BF16)],
        [SMEM] + [VMEM] * 3,
        (2 * ZPOS * D * KVW, 10 << 20, 0),
    )(c, acc, prompt_hidden, gprompt)
    parts = call(
        core_weight_kernel, shaped((SPLIT * HD, DZ), BF16), [VMEM] * 2, (0, 5 << 20, 0)
    )(mine, swap(send))
    parts = lax.all_to_all(parts, ("x", "zl"), 0, 0, tiled=True)
    rows = call(row_weight_kernel, shaped((DZ, HD), BF16), [VMEM], small)(parts)
    rows = lax.all_to_all(after(rows, grad_queries), ("y", "zh"), 0, 0, tiled=True)
    mine, send = call(
        head_weight_kernel, [shaped((OUT_ROWS, KVH * HD), F32)] * 2, [SMEM, VMEM], small
    )(c, rows)
    grad_weights = call(
        final_kernel, shaped((OUT_ROWS, 2 * KVH * HD), F32), [SMEM] + [VMEM] * 2, small
    )(c, mine, swap(send))
    return grad_queries, grad_weights


def solution(mesh):
    inner = Mesh(mesh.devices.reshape(NX, NZL, NY, NZH, NC), ("x", "zl", "y", "zh", "c"))
    prompt, resp = ("x", "zl"), ("y", "zh", "c")
    three, four = P(prompt, resp, None), P(prompt, resp, None, None)
    return jax.shard_map(
        body,
        mesh=inner,
        in_specs=(three, three, three, four, four, four, four, four, P(prompt, resp), P(prompt, resp)),
        out_specs=(four, P(prompt + resp, None)),
        check_vma=False,
    )
```

```python
import functools

import jax
import jax.numpy as jnp
from jax import lax
from jax.experimental import pallas as pl
from jax.experimental.pallas import tpu as pltpu
from jax.sharding import Mesh, PartitionSpec as P

D = 5120
QH = 32
KVH = 4
HD = 128
RLEN = 96
PPOS = 64
GROUP = QH // KVH
ROWS = GROUP * RLEN
META = 16
NX, NZL, NY, NZH, NC = 4, 2, 4, 4, 2
N_RESP = NY * NZH * NC
DX = D // NX
KVW = 2 * HD
ZPOS = NY * PPOS
OUT_ROWS = 20
F32 = jnp.float32
BF16 = jnp.bfloat16
VMEM = pl.BlockSpec(memory_space=pltpu.VMEM)
SMEM = pl.BlockSpec(memory_space=pltpu.SMEM)


def shaped(shape, dtype):
    return jax.ShapeDtypeStruct(shape, dtype)


def call(kernel, outs, specs, cost, scratch=(), limit=28):
    flops, nbytes, trans = cost
    return pl.pallas_call(
        kernel,
        name=kernel.__name__.replace("_kernel", ""),
        out_shape=outs,
        in_specs=specs,
        out_specs=jax.tree.map(lambda _: VMEM, outs),
        scratch_shapes=list(scratch),
        compiler_params=pltpu.CompilerParams(vmem_limit_bytes=limit * 1024 * 1024),
        cost_estimate=pl.CostEstimate(flops=flops, bytes_accessed=nbytes, transcendentals=trans),
    )


def pack_kernel(y_ref, rw_ref, ln_ref, pk_ref, pv_ref, rk_ref, rv_ref, q_ref, g_ref, *refs):
    kv, qd, sem = refs[:NY], refs[NY:2 * NY], refs[2 * NY]
    y = y_ref[0]
    wide = GROUP * HD
    low, high = pl.ds(0, HD), pl.ds(HD, HD)
    copies = []

    def copy(source, target):
        moved = pltpu.make_async_copy(source, target, sem.at[len(copies)])
        moved.start()
        copies.append(moved)

    for k in (1, 3, 2, 0):
        cols = pl.ds(pl.multiple_of(lax.rem(y + k, NY) * HD, HD), HD)
        copy(pk_ref.at[0, :, cols], kv[k].at[pl.ds(0, PPOS), low])
        copy(pv_ref.at[0, :, cols], kv[k].at[pl.ds(0, PPOS), high])
        copy(rk_ref.at[0, 0, :, cols], kv[k].at[pl.ds(PPOS, RLEN), low])
        copy(rv_ref.at[0, 0, :, cols], kv[k].at[pl.ds(PPOS, RLEN), high])
    for k in (1, 3, 2, 0):
        cols = pl.ds(pl.multiple_of(lax.rem(y + k, NY) * wide, HD), wide)
        copy(q_ref.at[0, 0, :, cols], qd[k].at[pl.ds(0, RLEN), :])
        copy(g_ref.at[0, 0, :, cols], qd[k].at[pl.ds(RLEN, RLEN), :])
    reward = jnp.full((META, KVW), rw_ref[0, 0], F32)
    top = reward.astype(BF16)
    rest = reward - top.astype(F32)
    mid = rest.astype(BF16)
    tail = rest - mid.astype(F32)
    lane = lax.broadcasted_iota(jnp.int32, (META, KVW), 1)
    length = jnp.full((META, KVW), ln_ref[0, 0].astype(F32), F32)
    meta = jnp.where(lane == 0, top.astype(F32), 0.0)
    meta = jnp.where(lane == 1, mid.astype(F32), meta)
    meta = jnp.where(lane == 2, tail, meta)
    meta = jnp.where(lane == 3, length, meta).astype(BF16)
    for k in range(NY):
        kv[k][PPOS + RLEN:, :] = meta
    for moved in copies:
        moved.wait()


def pack_z_kernel(*refs):
    ins, out = refs[:NY], refs[NY]
    row = lax.broadcasted_iota(jnp.int32, (META, KVW), 0)
    meta = jnp.zeros((META, KVW), F32)
    for k in range(NY):
        out[k * PPOS:(k + 1) * PPOS, :] = ins[k][0:PPOS, :]
        meta = jnp.where(row == k, ins[k][PPOS + RLEN:, :].astype(F32), meta)
    out[ZPOS:, :] = meta.astype(BF16)


def nt(a, b):
    return lax.dot_general(a, b, (((1,), (1,)), ((), ())), preferred_element_type=F32)


def nn(a, b):
    return lax.dot_general(a, b, (((1,), (0,)), ((), ())), preferred_element_type=F32)


def tn(a, b):
    return lax.dot_general(a, b, (((0,), (0,)), ((), ())), preferred_element_type=F32)


NT = 2 * NZH


def attention_kernel(*refs):
    kv = refs[0:NT]
    own = refs[NT:NT + NY]
    qd = refs[NT + NY:NT + 2 * NY]
    dq_refs = refs[NT + 2 * NY:NT + 3 * NY]
    gown_ref, gmine_ref, gother_ref = refs[NT + 3 * NY:NT + 3 * NY + 3]
    s_ref, dp_ref, q_ref, do_ref, kt_ref, acc_ref = refs[NT + 3 * NY + 3:]
    scale = HD ** (-0.5)
    log2e = 1.4426950408889634

    lane = lax.broadcasted_iota(jnp.int32, (META, HD), 1)
    row = lax.broadcasted_iota(jnp.int32, (META, HD), 0)
    total = jnp.zeros((1, 1), F32)
    squares = jnp.zeros((1, 1), F32)
    for t in range(NT):
        meta = kv[t][ZPOS:, 0:HD].astype(F32)
        rewards = jnp.sum(jnp.where((lane < 3) & (row < NY), meta, 0.0), axis=1, keepdims=True)
        total = total + jnp.sum(rewards, axis=0, keepdims=True)
        squares = squares + jnp.sum(rewards * rewards, axis=0, keepdims=True)
    mean = total / N_RESP
    spread = squares / N_RESP - mean * mean
    inverse = 1.0 / jnp.sqrt(jnp.maximum(spread, 0.5))

    for t in range(NT):
        kt_ref[:, t * ZPOS:(t + 1) * ZPOS] = kv[t][0:ZPOS, 0:HD].T

    own_start = NT * ZPOS
    key_index = lax.broadcasted_iota(jnp.int32, (RLEN, ROWS), 0)
    row_index = lax.rem(lax.broadcasted_iota(jnp.int32, (RLEN, ROWS), 1), RLEN)
    position = lax.broadcasted_iota(jnp.int32, (RLEN, HD), 0).astype(F32)

    for j in range(NY):
        meta = own[j][PPOS + RLEN:, 0:HD].astype(F32)
        reward = jnp.sum(jnp.where(lane < 3, meta, 0.0), axis=1, keepdims=True)[0:1]
        length = jnp.sum(jnp.where(lane == 3, meta, 0.0), axis=1, keepdims=True)[0:1]
        weight = (reward - mean) * inverse * RLEN / length
        live = position < length
        for h in range(GROUP):
            cols = slice(h * HD, (h + 1) * HD)
            rows = slice(h * RLEN, (h + 1) * RLEN)
            q_ref[rows, :] = qd[j][0:RLEN, cols]
            grad = qd[j][RLEN:2 * RLEN, cols].astype(F32)
            do_ref[rows, :] = jnp.where(live, grad * weight, 0.0).astype(BF16)
        kt_ref[:, own_start:own_start + RLEN] = own[j][PPOS:PPOS + RLEN, 0:HD].T
        q = q_ref[...]
        do = do_ref[...]
        mask = (key_index <= row_index) & (key_index.astype(F32) < length)

        tiles = [(kv[t], 0, ZPOS, t * ZPOS) for t in range(NT)]
        tiles.append((own[j], PPOS, RLEN, own_start))
        top = None
        for ref, start, size, at in tiles:
            s = nt(ref[start:start + size, 0:HD], q)
            if at == own_start:
                s = jnp.where(mask, s, -jnp.inf)
            s_ref[at:at + size, :] = s
            part = jnp.max(s, axis=0, keepdims=True)
            top = part if top is None else jnp.maximum(top, part)
        factor = scale * log2e
        top = top * factor
        norm = jnp.zeros((1, ROWS), F32)
        delta = jnp.zeros((1, ROWS), F32)
        for ref, start, size, at in tiles:
            p = jnp.exp2(s_ref[at:at + size, :] * factor - top)
            s_ref[at:at + size, :] = p
            dp = nt(ref[start:start + size, HD:KVW], do)
            dp_ref[at:at + size, :] = dp
            norm = norm + jnp.sum(p, axis=0, keepdims=True)
            delta = delta + jnp.sum(p * dp, axis=0, keepdims=True)
        inv = 1.0 / norm
        delta = delta * inv
        dq = jnp.zeros((HD, ROWS), F32)
        for ref, start, size, at in tiles:
            p = s_ref[at:at + size, :] * inv
            ds = (p * (dp_ref[at:at + size, :] - delta)).astype(BF16)
            dk = nn(ds, q) * scale
            dv = nn(p.astype(BF16), do)
            dq = dq + nn(kt_ref[:, at:at + size], ds)
            if at == own_start:
                gown_ref[j * RLEN:(j + 1) * RLEN, 0:HD] = dk.astype(BF16)
                gown_ref[j * RLEN:(j + 1) * RLEN, HD:KVW] = dv.astype(BF16)
            elif j == 0:
                acc_ref[at:at + size, 0:HD] = dk
                acc_ref[at:at + size, HD:KVW] = dv
            else:
                acc_ref[at:at + size, 0:HD] += dk
                acc_ref[at:at + size, HD:KVW] += dv
        dq = (dq * scale).T
        for h in range(GROUP):
            dq_refs[j][:, h * HD:(h + 1) * HD] = dq[h * RLEN:(h + 1) * RLEN, :].astype(BF16)
    half = NZH * ZPOS
    gmine_ref[...] = acc_ref[0:half, :].astype(BF16)
    gother_ref[...] = acc_ref[half:, :].astype(BF16)


def attention(kv, own, qd):
    keys = NT * ZPOS + RLEN
    pairs = NY * ROWS * keys
    outs = [shaped((RLEN, GROUP * HD), BF16)] * NY + [
        shaped((NY * RLEN, KVW), BF16),
        shaped((NZH * ZPOS, KVW), BF16),
        shaped((NZH * ZPOS, KVW), BF16),
    ]
    scratch = [
        pltpu.VMEM((keys, ROWS), F32),
        pltpu.VMEM((keys, ROWS), F32),
        pltpu.VMEM((ROWS, HD), BF16),
        pltpu.VMEM((ROWS, HD), BF16),
        pltpu.VMEM((HD, keys + 32), BF16),
        pltpu.VMEM((NT * ZPOS, KVW), F32),
    ]
    return call(
        attention_kernel, outs, [VMEM] * (NT + 2 * NY), (pairs * HD, 6 << 20, 0), scratch
    )(*kv, *own, *qd)


def core_sum_kernel(mine_ref, got_ref, *outs):
    for k in range(NZH):
        rows = slice(k * ZPOS, (k + 1) * ZPOS)
        outs[k][...] = (mine_ref[rows, :].astype(F32) + got_ref[rows, :].astype(F32)).astype(BF16)


def sum_kernel(*refs):
    ins, out = refs[:-1], refs[-1]
    total = ins[0][...].astype(F32)
    for ref in ins[1:]:
        total = total + ref[...].astype(F32)
    out[...] = total.astype(out.dtype)


HALF = (PPOS + RLEN) // 2


def own_weight_kernel(*refs):
    lows, highs = refs[:NY], refs[NY:2 * NY]
    grads_ref, acc_ref, prompt_ref, own_ref = refs[2 * NY:]
    split = HALF - PPOS
    for k in range(NY):
        own_ref[k * RLEN:k * RLEN + split, :] = lows[k][PPOS:, :]
        own_ref[k * RLEN + split:(k + 1) * RLEN, :] = highs[k][...]
        prompt_ref[k * PPOS:(k + 1) * PPOS, :] = lows[k][0:PPOS, :]
    grads = grads_ref[...]
    for i in range(NX):
        cols = slice(i * DX, (i + 1) * DX)
        acc_ref[:, cols] = tn(grads, own_ref[:, cols])


def prompt_weight_kernel(c_ref, acc_ref, hidden_ref, grads_ref, mine_ref, send_ref):
    first = c_ref[0] == 0
    grads = grads_ref[...]
    for i in range(NX):
        cols = slice(i * DX, (i + 1) * DX)
        total = acc_ref[:, cols] + tn(grads, hidden_ref[:, cols])
        low, high = total[0:HD], total[HD:KVW]
        mine_ref[:, cols] = jnp.where(first, low, high)
        send_ref[:, cols] = jnp.where(first, high, low).astype(BF16)


SPLIT = NX * NZL
DZ = D // SPLIT


def core_weight_kernel(mine_ref, got_ref, out):
    for k in range(SPLIT):
        cols = slice(k * DZ, (k + 1) * DZ)
        out[k * HD:(k + 1) * HD, :] = (mine_ref[:, cols] + got_ref[:, cols].astype(F32)).astype(BF16)


PAIR = NC * OUT_ROWS


def row_weight_kernel(in_ref, out):
    total = in_ref[0:HD, :].astype(F32)
    for i in range(1, SPLIT):
        total = total + in_ref[i * HD:(i + 1) * HD, :].astype(F32)
    out[...] = total.T.astype(BF16)


def head_weight_kernel(c_ref, in_ref, mine_ref, send_ref):
    first = c_ref[0] == 0
    terms = in_ref[...].astype(F32)
    for h in range(NY):
        total = jnp.zeros((PAIR, HD), F32)
        for zh in range(NZH):
            at = (h * NZH + zh) * PAIR
            total = total + terms[at:at + PAIR, :]
        total = total * (1.0 / (NX * NZL * N_RESP))
        low, high = total[0:OUT_ROWS, :], total[OUT_ROWS:PAIR, :]
        cols = slice(h * HD, (h + 1) * HD)
        mine_ref[:, cols] = jnp.where(first, low, high)
        send_ref[:, cols] = jnp.where(first, high, low)


def final_kernel(c_ref, mine_ref, got_ref, out):
    first = c_ref[0] == 0
    mine, got = mine_ref[...], got_ref[...]
    out[:, 0:KVH * HD] = jnp.where(first, mine, got)
    out[:, KVH * HD:] = jnp.where(first, got, mine)


def queries_kernel(y_ref, *refs):
    ins, out = refs[:NY], refs[NY]
    y = y_ref[0]
    wide = GROUP * HD
    for k in range(NY):
        at = lax.rem(y + k, NY) * wide
        out[0, 0, :, pl.ds(pl.multiple_of(at, HD), wide)] = ins[k][...]


def shift(value, axis, size, step):
    if step % size == 0:
        return value
    return lax.ppermute(value, axis, [(i, (i + step) % size) for i in range(size)])


def swap(value):
    return shift(value, "c", NC, 1)


def body(ph, pk, pv, rh, rq, rk, rv, go, rw, ln):
    index = lambda name: lax.axis_index(name).astype(jnp.int32).reshape(1)
    y, c = index("y"), index("c")
    after = lambda values, *others: lax.optimization_barrier((values, others))[0]
    small = (0, 1 << 20, 0)

    packs = call(
        pack_kernel,
        [shaped((PPOS + RLEN + META, KVW), BF16)] * NY + [shaped((2 * RLEN, GROUP * HD), BF16)] * NY,
        [SMEM] * 3 + [pl.BlockSpec(memory_space=pltpu.HBM)] * 6,
        small,
        [pltpu.SemaphoreType.DMA((6 * NY,))],
        limit=58,
    )(y, rw, ln, pk, pv, rk, rv, rq, go)
    kv_packs, qd_packs = packs[:NY], packs[NY:]
    own = [shift(kv_packs[k], "y", NY, k) for k in range(NY)]
    qd = [shift(qd_packs[k], "y", NY, k) if k != 2 else None for k in range(NY)]
    kvz = call(pack_z_kernel, shaped((ZPOS + META, KVW), BF16), [VMEM] * NY, small)(
        *after(own, qd[1], qd[3])
    )
    zpieces = [shift(kvz, "zh", NZH, k) for k in range(NZH)]
    qd[2] = shift(after(qd_packs[2], own, qd[1], qd[3]), "y", NY, 2)
    cpieces = [swap(piece) for piece in zpieces]
    low = jnp.concatenate([ph[0], rh[0, 0, :HALF - PPOS]], axis=0)
    low, high = after((low, rh[0, 0, HALF - PPOS:]), qd[2], zpieces[1:])
    low_left, high_right = shift(low, "y", NY, 1), shift(high, "y", NY, -1)
    low_right, high_left = shift(low, "y", NY, -1), shift(high, "y", NY, 1)

    *dq, gown, gmine, gother = attention(zpieces + cpieces, own, qd)
    far_low, far_high = after((low_left, high_right), gother)
    far_low, far_high = shift(far_low, "y", NY, 1), shift(far_high, "y", NY, -1)
    got = swap(gother)
    sums = call(core_sum_kernel, [shaped((ZPOS, KVW), BF16)] * NZH, [VMEM] * 2, small)(gmine, got)
    back = [shift(sums[k], "zh", NZH, -k) for k in range(NZH)]
    acc, prompt_hidden = call(
        own_weight_kernel,
        [shaped((KVW, D), F32), shaped((ZPOS, D), BF16)],
        [VMEM] * (2 * NY + 1),
        (2 * NY * RLEN * D * KVW, 12 << 20, 0),
        [pltpu.VMEM((NY * RLEN, D), BF16)],
    )(low, low_left, far_low, low_right, high, high_left, far_high, high_right, gown)
    gprompt = call(sum_kernel, shaped((ZPOS, KVW), BF16), [VMEM] * NZH, small)(*after(back, acc))

    dq_back = [shift(dq[k] if k != 2 else after(dq[k], gprompt), "y", NY, -k) for k in range(NY)]
    grad_queries = call(
        queries_kernel, shaped((1, 1, RLEN, QH * HD), BF16), [SMEM] + [VMEM] * NY, small
    )(y, *dq_back)

    mine, send = call(
        prompt_weight_kernel,
        [shaped((HD, D), F32), shaped((HD, D), BF16)],
        [SMEM] + [VMEM] * 3,
        (2 * ZPOS * D * KVW, 10 << 20, 0),
    )(c, acc, prompt_hidden, gprompt)
    parts = call(
        core_weight_kernel, shaped((SPLIT * HD, DZ), BF16), [VMEM] * 2, (0, 5 << 20, 0)
    )(mine, swap(send))
    parts = lax.all_to_all(parts, ("x", "zl"), 0, 0, tiled=True)
    rows = call(row_weight_kernel, shaped((DZ, HD), BF16), [VMEM], small)(parts)
    rows = lax.all_to_all(after(rows, grad_queries), ("y", "zh"), 0, 0, tiled=True)
    mine, send = call(
        head_weight_kernel, [shaped((OUT_ROWS, KVH * HD), F32)] * 2, [SMEM, VMEM], small
    )(c, rows)
    grad_weights = call(
        final_kernel, shaped((OUT_ROWS, 2 * KVH * HD), F32), [SMEM] + [VMEM] * 2, small
    )(c, mine, swap(send))
    return grad_queries, grad_weights


def solution(mesh):
    inner = Mesh(mesh.devices.reshape(NX, NZL, NY, NZH, NC), ("x", "zl", "y", "zh", "c"))
    prompt, resp = ("x", "zl"), ("y", "zh", "c")
    three, four = P(prompt, resp, None), P(prompt, resp, None, None)
    return jax.shard_map(
        body,
        mesh=inner,
        in_specs=(three, three, three, four, four, four, four, four, P(prompt, resp), P(prompt, resp)),
        out_specs=(four, P(prompt + resp, None)),
        check_vma=False,
    )
```
